32 devices in a mesh: rep: 8 (over z, y), tp: 4 (over x, core).
Axes of the slice: x: 2, y: 2, z: 4, core: 2. Of those that a mesh axis runs over, the one named last changes fastest.
Arguments:
- reference_rows: bfloat16 [2048, 8192], P('rep', 'tp'), may hold values from -7 to 7
- critic_rows: bfloat16 [2048, 4096], P('rep', 'tp'), may hold values from -7 to 7
- segment_ids: int32 [2048], P('rep'), may hold values from -1 to 2047, as said below
- pack_dest: int32 [8, 8], P('rep'), may hold values from 0 to 7, as said below
- ref_query: bfloat16 [8192, 4096], P('rep', 'tp'), may hold values from -2 to 2
- ref_key: bfloat16 [8192, 1024], P('rep', 'tp'), may hold values from -2 to 2
- ref_value: bfloat16 [8192, 1024], P('rep', 'tp'), may hold values from -0.0625 to 0.0625
- critic_query: bfloat16 [4096, 4096], P(None, 'tp'), may hold values from -2 to 2
- critic_key: bfloat16 [4096, 1024], P(None, 'tp'), may hold values from -2 to 2
- critic_value: bfloat16 [4096, 1024], P(None, 'tp'), may hold values from -0.09375 to 0.09375
- ref_readout: bfloat16 [4096], P('tp'), may hold values from -0.09375 to 0.09375
- critic_readout: bfloat16 [4096], P('tp'), may hold values from -0.09375 to 0.09375
Outputs:
- ref_score: float32 [2048], P('rep')
- value: float32 [2048], P('rep')
The draws below stay inside these ranges and needn't reach their ends.
Inputs may be any that keep to these rules, and one draw needn't show every extreme that they name: Each row is a permutation: block b of replica s goes to pack pack_dest[s, b]. `segment_ids`: in every aligned block of 32 slots the used rows come first and the rest hold -1; a block holds 1 to 31 used rows, and every pack receives exactly 31 used rows from some replica and exactly 128 used rows in all. A rollout is a run of consecutive used rows with one id inside one block; different rollouts have different ids.
All inputs are finite; a program needn't handle non-finite values.
Results may differ from the reference program's by a relative error of at most 0.0084.
Values may be sent and summed in bfloat16 or wider, within the bound.
A program may use at most 128 MiB of HBM per device.

```python
import jax
import jax.numpy as jnp
from jax import lax

DR = 8192
HR = 32
KR = 8
DC = 4096
HC = 32
KC = 8
HD = 128
CAP = 16
PACK = 128
TOKENS = 2048


def shared_plan(key):
    replicas = PACK // CAP
    base = jax.random.fold_in(key, 11)
    streams = jax.random.split(base, 6)
    orders = jax.vmap(lambda single: jax.random.permutation(single, replicas))(jax.random.split(streams[0], replicas)).astype(jnp.int32)
    reach = jax.random.randint(streams[1], (replicas, 1), 0, CAP)
    spread = jax.random.randint(streams[2], (replicas, replicas), 0, CAP * 64) % (reach + 1)
    leader = jax.random.randint(streams[3], (replicas,), 0, replicas)
    offsets = jax.random.randint(streams[4], (replicas,), 1, replicas)
    columns = jnp.arange(replicas)
    spread = spread.at[leader, columns].set(CAP - 1)
    spread = spread.at[(leader + offsets) % replicas, columns].set(0)
    partner = (jnp.arange(replicas)[:, None] + offsets[None, :]) % replicas
    used = CAP + spread - jnp.take_along_axis(spread, partner, axis=0)
    used_blocks = jnp.take_along_axis(used, orders, axis=1)
    starts = jax.random.randint(streams[5], (replicas, replicas, 2 * CAP), 0, 64) == 0
    starts = starts.at[:, :, 0].set(True)
    slots = jnp.arange(2 * CAP)
    live = slots[None, None, :] < used_blocks[:, :, None]
    live_starts = (starts & live).astype(jnp.int32)
    within = jnp.cumsum(live_starts, axis=-1) - 1
    count = jnp.sum(live_starts, axis=-1, keepdims=True)
    block_base = (jnp.arange(replicas)[:, None] * replicas + jnp.arange(replicas)[None, :]) * (2 * CAP)
    idents = block_base[:, :, None] + 2 * CAP - count + within
    segments = jnp.where(live, idents, -1)
    return (orders, segments.reshape(-1).astype(jnp.int32))


def draw_pack_dest(key, part):
    return shared_plan(key)[0]


def draw_segment_ids(key, part):
    return shared_plan(key)[1]


def tilted_weight(key, salt, rows_count, columns):
    base_draw = jax.random.truncated_normal(jax.random.fold_in(key, salt), -4.0, 4.0, (rows_count, columns), jnp.float32)
    result = base_draw * float(rows_count) ** (-0.5)
    return result


def drawn_rows(key, salt, width):
    result = jax.random.truncated_normal(jax.random.fold_in(key, salt), -5.0, 5.0, (TOKENS, width), jnp.float32)
    return result


def draw_reference_rows(key, part):
    return drawn_rows(key, 61, DR).astype(jnp.bfloat16)


def draw_critic_rows(key, part):
    return drawn_rows(key, 62, DC).astype(jnp.bfloat16)


def draw_ref_query(key, part):
    return tilted_weight(key, 51, DR, HR * HD).astype(jnp.bfloat16)


def draw_ref_key(key, part):
    return tilted_weight(key, 52, DR, KR * HD).astype(jnp.bfloat16)


def draw_critic_query(key, part):
    return tilted_weight(key, 53, DC, HC * HD).astype(jnp.bfloat16)


def draw_critic_key(key, part):
    return tilted_weight(key, 54, DC, KC * HD).astype(jnp.bfloat16)


def levels(key, extent, cuts, low, top_value):
    level = 1.0
    for dim, blocks in cuts:
        heights = jax.random.uniform(jax.random.fold_in(jax.random.fold_in(key, 6), dim), (blocks,), jnp.float32, low / len(cuts), top_value / len(cuts))
        level = level * jnp.repeat(jnp.exp(heights), extent[dim] // blocks).reshape((-1,) + (1,) * (len(extent) - 1 - dim))
    return level


def gaussian(rng, dims, scale, bound, cuts=(), kind=jnp.bfloat16):
    array = jax.random.normal(rng, dims, jnp.float32) * scale
    if len(cuts) > 0:
        array = levels(rng, dims, cuts, -0.22, 0.18) * array
    return jnp.clip(array, min=-bound, max=bound).astype(kind)


def setup_inputs(seed: int = 0) -> dict:
    arg_keys = jax.random.split(jax.random.key(seed), 13)
    return {
        "reference_rows": draw_reference_rows(jax.random.fold_in(arg_keys[12], 71), 0),
        "critic_rows": draw_critic_rows(jax.random.fold_in(arg_keys[12], 71), 0),
        "segment_ids": draw_segment_ids(jax.random.fold_in(arg_keys[12], 71), 0),
        "pack_dest": draw_pack_dest(jax.random.fold_in(arg_keys[12], 71), 0),
        "ref_query": draw_ref_query(jax.random.fold_in(arg_keys[12], 71), 0),
        "ref_key": draw_ref_key(jax.random.fold_in(arg_keys[12], 71), 0),
        "ref_value": gaussian(arg_keys[6], (DR, KR * HD), DR ** -0.5, 0.0625, ((0, 8), (1, 4))),
        "critic_query": draw_critic_query(jax.random.fold_in(arg_keys[12], 71), 0),
        "critic_key": draw_critic_key(jax.random.fold_in(arg_keys[12], 71), 0),
        "critic_value": gaussian(arg_keys[9], (DC, KC * HD), DC ** -0.5, 0.09375, ((1, 4),)),
        "ref_readout": gaussian(arg_keys[10], (HR * HD,), (HR * HD) ** -0.5, 0.09375, ((0, 4),)),
        "critic_readout": gaussian(arg_keys[11], (HC * HD,), (HC * HD) ** -0.5, 0.09375, ((0, 4),)),
    }


def normalize(source):
    widened = source.astype(jnp.float32)
    scale_row = lax.rsqrt(lax.optimization_barrier(jnp.mean(widened * widened, axis=-1, keepdims=True)) + 1e-05)
    return (widened * scale_row).astype(jnp.bfloat16)

def attend(queries, keys_in, values_in, segments):
    row_count = queries.shape[0]
    groups = keys_in.shape[1] // HD
    shared = queries.shape[1] // keys_in.shape[1]
    query_four = queries.astype(jnp.float32).reshape(row_count, groups, shared, HD)
    key_three = keys_in.astype(jnp.float32).reshape(row_count, groups, HD)
    value_three = values_in.astype(jnp.float32).reshape(row_count, groups, HD)
    scores = jnp.einsum('pgjd,qgd->gjpq', query_four, key_three) * HD ** (-0.5)
    position = jnp.arange(row_count)
    allowed = (position[None, :] <= position[:, None]) & (segments[:, None] == segments[None, :])
    masked = jnp.where(allowed, scores, -1e+30)
    row_max = lax.optimization_barrier(jnp.max(masked, axis=-1, keepdims=True))
    powers = jnp.where(allowed, jnp.exp(masked - row_max), 0.0)
    weights = (powers / lax.optimization_barrier(jnp.sum(powers, axis=-1, keepdims=True))).astype(jnp.bfloat16)
    mixture = jnp.einsum('gjpq,qgd->pgjd', weights.astype(jnp.float32), value_three)
    return mixture.reshape(row_count, groups * shared * HD).astype(jnp.bfloat16)

def section(rows_in, segments, w_query, w_key, w_value):
    normed = normalize(rows_in)
    queries = jnp.dot(normed, w_query, preferred_element_type=jnp.float32).astype(jnp.bfloat16)
    keys_in = jnp.dot(normed, w_key, preferred_element_type=jnp.float32).astype(jnp.bfloat16)
    values_in = jnp.dot(normed, w_value, preferred_element_type=jnp.float32).astype(jnp.bfloat16)
    return attend(queries, keys_in, values_in, segments)

def compact_index(segments):
    row_count = segments.shape[0]
    sort_keys = jnp.where(segments >= 0, 0, row_count).astype(jnp.int32) + jnp.arange(row_count, dtype=jnp.int32)
    return jnp.argsort(sort_keys)[:row_count // 2].astype(jnp.int32)

def reference(reference_rows, critic_rows, segment_ids, pack_dest, ref_query, ref_key, ref_value, critic_query, critic_key, critic_value, ref_readout, critic_readout):
    replicas = pack_dest.shape[0]
    block_rows = 2 * CAP
    inverse = jnp.argsort(pack_dest, axis=1).astype(jnp.int32)

    def to_packs(source):
        rest = source.shape[1:]
        blocks = source.reshape((replicas, replicas, block_rows) + rest)
        index_shape = (replicas, replicas) + (1,) * (1 + len(rest))
        picked = jnp.take_along_axis(blocks, inverse.reshape(index_shape), axis=1)
        return jnp.swapaxes(picked, 0, 1).reshape((replicas, replicas * block_rows) + rest)
    ref_packs = to_packs(reference_rows)
    critic_packs = to_packs(critic_rows)
    id_packs = to_packs(segment_ids)

    def one_pack(inputs):
        ref_pack, critic_pack, id_pack = inputs
        chosen = compact_index(id_pack)
        pack_ids = id_pack[chosen]
        ref_attn = section(ref_pack[chosen], pack_ids, ref_query, ref_key, ref_value)
        critic_attn = section(critic_pack[chosen], pack_ids, critic_query, critic_key, critic_value)
        ref_part = jnp.dot(ref_attn, ref_readout, preferred_element_type=jnp.float32)
        critic_part = jnp.dot(critic_attn, critic_readout, preferred_element_type=jnp.float32)
        pack_scores = jnp.stack([ref_part, critic_part])
        expanded = jnp.zeros((2, id_pack.shape[0]), jnp.float32)
        return expanded.at[:, chosen].set(pack_scores)
    results = lax.map(one_pack, (ref_packs, critic_packs, id_packs))
    returned = results.reshape(replicas, 2, replicas, block_rows).transpose(2, 1, 0, 3)
    ordered = jnp.take_along_axis(returned, pack_dest.reshape(replicas, 1, replicas, 1), axis=2)
    used = segment_ids.reshape(replicas, 1, replicas, block_rows) >= 0
    ordered = jnp.where(used, ordered, 0.0)
    return (ordered[:, 0].reshape(-1), ordered[:, 1].reshape(-1))
```

```python
import jax
import jax.numpy as jnp
from jax import lax
from jax.sharding import PartitionSpec as P

HD = 128


def attend(queries, keys_in, values_in, segments):
    row_count = queries.shape[0]
    groups = keys_in.shape[1] // HD
    shared = queries.shape[1] // keys_in.shape[1]
    query_four = queries.reshape(row_count, groups, shared, HD)
    key_three = keys_in.reshape(row_count, groups, HD)
    value_three = values_in.reshape(row_count, groups, HD)
    scores = jnp.einsum(
        "pgjd,qgd->gjpq", query_four, key_three, preferred_element_type=jnp.float32
    ) * HD ** (-0.5)
    position = jnp.arange(row_count)
    allowed = (position[None, :] <= position[:, None]) & (segments[:, None] == segments[None, :])
    masked = jnp.where(allowed, scores, -1e30)
    row_max = jnp.max(masked, axis=-1, keepdims=True)
    powers = jnp.where(allowed, jnp.exp(masked - row_max), 0.0)
    weights = (powers / jnp.sum(powers, axis=-1, keepdims=True)).astype(jnp.bfloat16)
    mixture = jnp.einsum("gjpq,qgd->pgjd", weights, value_three, preferred_element_type=jnp.float32)
    return mixture.reshape(row_count, groups * shared * HD).astype(jnp.bfloat16)


def project(rows, weight):
    return jnp.dot(rows, weight, preferred_element_type=jnp.float32)


def tables(ids_all, dest_all):
    replicas = dest_all.shape[0]
    goes = dest_all[:, :, None] == jnp.arange(replicas)[None, None, :]
    inverse = jnp.sum(jnp.where(goes, jnp.arange(replicas)[None, :, None], 0), axis=1)
    ids_blocks = ids_all.reshape(replicas, replicas, -1)
    received = jnp.sum(
        jnp.where(goes[:, :, :, None], ids_blocks[:, :, None, :], 0), axis=1
    )
    received = jnp.transpose(received, (1, 0, 2)).reshape(replicas, -1)
    valid = received >= 0
    rank = jnp.cumsum(valid.astype(jnp.int32), axis=1) - 1
    return inverse, received, valid, rank


def body(
    reference_rows,
    critic_rows,
    segment_ids,
    pack_dest,
    ref_query,
    ref_key,
    ref_value,
    critic_query,
    critic_key,
    critic_value,
    ref_readout,
    critic_readout,
):
    replicas = lax.axis_size("rep")
    width = lax.axis_size("tp")
    me = lax.axis_index("rep")
    slot_count = segment_ids.shape[0]
    block_rows = slot_count // replicas
    rows_per_pack = slot_count // 2
    quarter = slot_count // width
    destination = pack_dest[0]

    info = lax.all_gather(jnp.concatenate([segment_ids, destination]), "rep", axis=0, tiled=False)
    wide_ref = reference_rows.astype(jnp.float32)
    squares = lax.all_gather(jnp.sum(wide_ref * wide_ref, axis=1), ("rep", "tp"), axis=0, tiled=False)

    split = lax.all_to_all(reference_rows, "tp", split_axis=0, concat_axis=1, tiled=True)
    slices = lax.all_to_all(split, "rep", split_axis=1, concat_axis=0, tiled=True)
    ref_slice = lax.all_gather(slices, "tp", axis=0, tiled=True)

    own_inverse = jnp.sum(
        jnp.where(
            destination[:, None] == jnp.arange(replicas)[None, :], jnp.arange(replicas)[:, None], 0
        ),
        axis=0,
    )
    blocks = critic_rows.reshape(replicas, block_rows, -1)
    critic_sent = jnp.take(blocks, own_inverse, axis=0).reshape(critic_rows.shape)
    critic_in = lax.all_to_all(critic_sent, "rep", split_axis=0, concat_axis=0, tiled=True)

    ids_all, dest_all = info[:, :slot_count], info[:, slot_count:]
    inverse, received, valid, rank = tables(ids_all, dest_all)
    place = (rank[:, None, :] == jnp.arange(rows_per_pack)[None, :, None]) & valid[:, None, :]
    position = jnp.arange(slot_count)
    sender = position // block_rows
    in_sender = jnp.transpose(inverse)[:, :, None] * block_rows + jnp.arange(block_rows)[None, None, :]
    in_sender = in_sender.reshape(replicas, slot_count)
    row_of = (in_sender // quarter) * (replicas * quarter) + sender[None, :] * quarter + in_sender % quarter
    order = jnp.sum(jnp.where(place, row_of[:, None, :], 0), axis=2).reshape(-1)

    mine = lambda table: lax.dynamic_index_in_dim(table, me, 0, keepdims=False)
    place_mine = mine(place)
    chosen = jnp.sum(jnp.where(place_mine, position[None, :], 0), axis=1)
    pack_ids = jnp.sum(jnp.where(place_mine, mine(received)[None, :], 0), axis=1)

    compact = jnp.take(ref_slice, order, axis=0)
    weight = jnp.concatenate([ref_query, ref_key, ref_value], axis=1)
    partial = project(compact, weight).astype(jnp.bfloat16)
    parts = lax.all_to_all(partial, "rep", split_axis=0, concat_axis=0, tiled=True)

    critic_full = lax.all_gather(critic_in[chosen], "tp", axis=1, tiled=True)
    widened = critic_full.astype(jnp.float32)
    scale_row = lax.rsqrt(jnp.mean(widened * widened, axis=-1, keepdims=True) + 1e-05)
    critic_normed = (widened * scale_row).astype(jnp.bfloat16)
    critic_attn = attend(
        project(critic_normed, critic_query).astype(jnp.bfloat16),
        project(critic_normed, critic_key).astype(jnp.bfloat16),
        project(critic_normed, critic_value).astype(jnp.bfloat16),
        pack_ids,
    )

    mean_square = jnp.sum(squares.reshape(replicas, width, slot_count), axis=1) / (
        reference_rows.shape[1] * width
    )
    goes_here = dest_all == me
    square_in = jnp.sum(
        jnp.where(goes_here[:, :, None], mean_square.reshape(replicas, replicas, block_rows), 0.0),
        axis=1,
    ).reshape(-1)
    square_rows = jnp.sum(jnp.where(place_mine, square_in[None, :], 0.0), axis=1)
    summed = jnp.sum(parts.reshape(replicas, rows_per_pack, -1).astype(jnp.float32), axis=0)
    ref_qkv = (summed * lax.rsqrt(square_rows + 1e-05)[:, None]).astype(jnp.bfloat16)
    nq, nk = ref_query.shape[1], ref_key.shape[1]
    ref_attn = attend(ref_qkv[:, :nq], ref_qkv[:, nq : nq + nk], ref_qkv[:, nq + nk :], pack_ids)

    terms = jnp.stack(
        [
            jnp.sum(ref_attn.astype(jnp.float32) * ref_readout.astype(jnp.float32), axis=1),
            jnp.sum(critic_attn.astype(jnp.float32) * critic_readout.astype(jnp.float32), axis=1),
        ]
    )
    spread = jnp.sum(jnp.where(place_mine[None, :, :], terms[:, :, None], 0.0), axis=1)
    everyone = lax.all_gather(spread, ("rep", "tp"), axis=0, tiled=False)
    everyone = everyone.reshape(replicas, width, 2, replicas, block_rows)
    back = lax.dynamic_index_in_dim(everyone, me, 3, keepdims=False)
    back = jnp.sum(back, axis=1)
    picked = destination[:, None] == jnp.arange(replicas)[None, :]
    home = jnp.sum(
        jnp.where(picked[:, :, None, None], back[None], 0.0), axis=1
    )
    home = jnp.transpose(home, (1, 0, 2)).reshape(2, slot_count)
    home = jnp.where(segment_ids[None, :] >= 0, home, 0.0)
    return (home[0], home[1])


def solution(mesh):
    return jax.shard_map(
        body,
        mesh=mesh,
        in_specs=(
            P("rep", "tp"),
            P("rep", "tp"),
            P("rep"),
            P("rep", None),
            P("rep", "tp"),
            P("rep", "tp"),
            P("rep", "tp"),
            P(None, "tp"),
            P(None, "tp"),
            P(None, "tp"),
            P("tp"),
            P("tp"),
        ),
        out_specs=(P("rep"), P("rep")),
        check_vma=False,
    )
```

```python
import jax
import jax.numpy as jnp
from jax import lax
from jax.sharding import PartitionSpec as P

HD = 128


def attend(queries, keys_in, values_in, segments):
    row_count = queries.shape[0]
    groups = keys_in.shape[1] // HD
    shared = queries.shape[1] // keys_in.shape[1]
    query_four = queries.reshape(row_count, groups, shared, HD)
    key_three = keys_in.reshape(row_count, groups, HD)
    value_three = values_in.reshape(row_count, groups, HD)
    scores = jnp.einsum(
        "pgjd,qgd->gjpq", query_four, key_three, preferred_element_type=jnp.float32
    ) * HD ** (-0.5)
    position = jnp.arange(row_count)
    allowed = (position[None, :] <= position[:, None]) & (segments[:, None] == segments[None, :])
    masked = jnp.where(allowed, scores, -1e30)
    row_max = jnp.max(masked, axis=-1, keepdims=True)
    powers = jnp.where(allowed, jnp.exp(masked - row_max), 0.0)
    weights = (powers / jnp.sum(powers, axis=-1, keepdims=True)).astype(jnp.bfloat16)
    mixture = jnp.einsum("gjpq,qgd->pgjd", weights, value_three, preferred_element_type=jnp.float32)
    return mixture.reshape(row_count, groups * shared * HD).astype(jnp.bfloat16)


def project(rows, weight):
    return jnp.dot(rows, weight, preferred_element_type=jnp.float32)


def tables(ids_all, dest_all):
    replicas = dest_all.shape[0]
    goes = dest_all[:, :, None] == jnp.arange(replicas)[None, None, :]
    inverse = jnp.sum(jnp.where(goes, jnp.arange(replicas)[None, :, None], 0), axis=1)
    ids_blocks = ids_all.reshape(replicas, replicas, -1)
    received = jnp.sum(
        jnp.where(goes[:, :, :, None], ids_blocks[:, :, None, :], 0), axis=1
    )
    received = jnp.transpose(received, (1, 0, 2)).reshape(replicas, -1)
    valid = received >= 0
    rank = jnp.cumsum(valid.astype(jnp.int32), axis=1) - 1
    return inverse, received, valid, rank


def body(
    reference_rows,
    critic_rows,
    segment_ids,
    pack_dest,
    ref_query,
    ref_key,
    ref_value,
    critic_query,
    critic_key,
    critic_value,
    ref_readout,
    critic_readout,
):
    replicas = lax.axis_size("rep")
    width = lax.axis_size("tp")
    me = lax.axis_index("rep")
    slot_count = segment_ids.shape[0]
    block_rows = slot_count // replicas
    rows_per_pack = slot_count // 2
    quarter = slot_count // width
    destination = pack_dest[0]

    info = lax.all_gather(jnp.concatenate([segment_ids, destination]), "rep", axis=0, tiled=False)
    wide_ref = reference_rows.astype(jnp.float32)
    squares = lax.psum(jnp.sum(wide_ref * wide_ref, axis=1), "tp")
    own_inverse = jnp.sum(
        jnp.where(
            destination[:, None] == jnp.arange(replicas)[None, :], jnp.arange(replicas)[:, None], 0
        ),
        axis=0,
    )
    squares_sent = jnp.take(squares.reshape(replicas, block_rows), own_inverse, axis=0)
    square_in = lax.all_to_all(squares_sent, "rep", split_axis=0, concat_axis=0, tiled=True).reshape(-1)
    info, square_in, reference_rows, critic_rows = lax.optimization_barrier(
        (info, square_in, reference_rows, critic_rows)
    )

    split = lax.all_to_all(reference_rows, "tp", split_axis=0, concat_axis=1, tiled=True)
    slices = lax.all_to_all(split, "rep", split_axis=1, concat_axis=0, tiled=True)
    ref_slice = lax.all_gather(slices, "tp", axis=0, tiled=True)

    blocks = critic_rows.reshape(replicas, block_rows, -1)
    critic_sent = jnp.take(blocks, own_inverse, axis=0).reshape(critic_rows.shape)
    critic_in = lax.all_to_all(critic_sent, "rep", split_axis=0, concat_axis=0, tiled=True)

    ids_all, dest_all = info[:, :slot_count], info[:, slot_count:]
    inverse, received, valid, rank = tables(ids_all, dest_all)
    place = (rank[:, None, :] == jnp.arange(rows_per_pack)[None, :, None]) & valid[:, None, :]
    position = jnp.arange(slot_count)
    sender = position // block_rows
    in_sender = jnp.transpose(inverse)[:, :, None] * block_rows + jnp.arange(block_rows)[None, None, :]
    in_sender = in_sender.reshape(replicas, slot_count)
    row_of = (in_sender // quarter) * (replicas * quarter) + sender[None, :] * quarter + in_sender % quarter
    order = jnp.sum(jnp.where(place, row_of[:, None, :], 0), axis=2).reshape(-1)

    mine = lambda table: lax.dynamic_index_in_dim(table, me, 0, keepdims=False)
    place_mine = mine(place)
    chosen = jnp.sum(jnp.where(place_mine, position[None, :], 0), axis=1)
    pack_ids = jnp.sum(jnp.where(place_mine, mine(received)[None, :], 0), axis=1)

    compact = jnp.take(ref_slice, order, axis=0)
    weight = jnp.concatenate([ref_query, ref_key, ref_value], axis=1)
    partial = project(compact, weight).astype(jnp.bfloat16)
    parts = lax.all_to_all(partial, "rep", split_axis=0, concat_axis=0, tiled=True)

    critic_full = lax.all_gather(critic_in[chosen], "tp", axis=1, tiled=True)
    widened = critic_full.astype(jnp.float32)
    scale_row = lax.rsqrt(jnp.mean(widened * widened, axis=-1, keepdims=True) + 1e-05)
    critic_normed = (widened * scale_row).astype(jnp.bfloat16)
    critic_attn = attend(
        project(critic_normed, critic_query).astype(jnp.bfloat16),
        project(critic_normed, critic_key).astype(jnp.bfloat16),
        project(critic_normed, critic_value).astype(jnp.bfloat16),
        pack_ids,
    )

    square_rows = jnp.sum(jnp.where(place_mine, square_in[None, :], 0.0), axis=1) / (
        reference_rows.shape[1] * width
    )
    summed = jnp.sum(parts.reshape(replicas, rows_per_pack, -1).astype(jnp.float32), axis=0)
    ref_qkv = (summed * lax.rsqrt(square_rows + 1e-05)[:, None]).astype(jnp.bfloat16)
    nq, nk = ref_query.shape[1], ref_key.shape[1]
    ref_attn = attend(ref_qkv[:, :nq], ref_qkv[:, nq : nq + nk], ref_qkv[:, nq + nk :], pack_ids)

    terms = jnp.stack(
        [
            jnp.sum(ref_attn.astype(jnp.float32) * ref_readout.astype(jnp.float32), axis=1),
            jnp.sum(critic_attn.astype(jnp.float32) * critic_readout.astype(jnp.float32), axis=1),
        ]
    )
    spread = jnp.sum(jnp.where(place_mine[None, :, :], terms[:, :, None], 0.0), axis=1)
    spread = lax.psum(spread, "tp").reshape(2, replicas, block_rows)
    sent = jnp.transpose(spread, (1, 0, 2)).reshape(replicas, 2 * block_rows)
    back = lax.all_to_all(sent, "rep", split_axis=0, concat_axis=0, tiled=True)
    back = back.reshape(replicas, 2, block_rows)
    picked = destination[:, None] == jnp.arange(replicas)[None, :]
    home = jnp.sum(
        jnp.where(picked[:, :, None, None], back[None], 0.0), axis=1
    )
    home = jnp.transpose(home, (1, 0, 2)).reshape(2, slot_count)
    home = jnp.where(segment_ids[None, :] >= 0, home, 0.0)
    return (home[0], home[1])


def solution(mesh):
    return jax.shard_map(
        body,
        mesh=mesh,
        in_specs=(
            P("rep", "tp"),
            P("rep", "tp"),
            P("rep"),
            P("rep", None),
            P("rep", "tp"),
            P("rep", "tp"),
            P("rep", "tp"),
            P(None, "tp"),
            P(None, "tp"),
            P(None, "tp"),
            P("tp"),
            P("tp"),
        ),
        out_specs=(P("rep"), P("rep")),
        check_vma=False,
    )
```

```python
import jax
import jax.numpy as jnp
from jax import lax
from jax.sharding import PartitionSpec as P

HD = 128


def attend(queries, keys_in, values_in, segments):
    row_count = queries.shape[0]
    groups = keys_in.shape[1] // HD
    shared = queries.shape[1] // keys_in.shape[1]
    query_four = queries.reshape(row_count, groups, shared, HD)
    key_three = keys_in.reshape(row_count, groups, HD)
    value_three = values_in.reshape(row_count, groups, HD)
    scores = jnp.einsum(
        "pgjd,qgd->gjpq", query_four, key_three, preferred_element_type=jnp.float32
    ) * HD ** (-0.5)
    position = jnp.arange(row_count)
    allowed = (position[None, :] <= position[:, None]) & (segments[:, None] == segments[None, :])
    masked = jnp.where(allowed, scores, -1e30)
    row_max = jnp.max(masked, axis=-1, keepdims=True)
    powers = jnp.where(allowed, jnp.exp(masked - row_max), 0.0)
    weights = (powers / jnp.sum(powers, axis=-1, keepdims=True)).astype(jnp.bfloat16)
    mixture = jnp.einsum("gjpq,qgd->pgjd", weights, value_three, preferred_element_type=jnp.float32)
    return mixture.reshape(row_count, groups * shared * HD).astype(jnp.bfloat16)


def project(rows, weight):
    return jnp.dot(rows, weight, preferred_element_type=jnp.float32)


def tables(ids_all, dest_all):
    replicas = dest_all.shape[0]
    goes = dest_all[:, :, None] == jnp.arange(replicas)[None, None, :]
    inverse = jnp.sum(jnp.where(goes, jnp.arange(replicas)[None, :, None], 0), axis=1)
    ids_blocks = ids_all.reshape(replicas, replicas, -1)
    received = jnp.sum(
        jnp.where(goes[:, :, :, None], ids_blocks[:, :, None, :], 0), axis=1
    )
    received = jnp.transpose(received, (1, 0, 2)).reshape(replicas, -1)
    valid = received >= 0
    rank = jnp.cumsum(valid.astype(jnp.int32), axis=1) - 1
    return inverse, received, valid, rank


def body(
    reference_rows,
    critic_rows,
    segment_ids,
    pack_dest,
    ref_query,
    ref_key,
    ref_value,
    critic_query,
    critic_key,
    critic_value,
    ref_readout,
    critic_readout,
):
    replicas = lax.axis_size("rep")
    width = lax.axis_size("tp")
    me = lax.axis_index("rep")
    slot_count = segment_ids.shape[0]
    block_rows = slot_count // replicas
    rows_per_pack = slot_count // 2
    quarter = slot_count // width
    destination = pack_dest[0]

    own_info = jnp.concatenate([segment_ids, destination])
    copies = jnp.broadcast_to(own_info[None, :], (replicas, own_info.shape[0]))
    info = lax.all_to_all(copies, "rep", split_axis=0, concat_axis=0, tiled=True)
    wide_ref = reference_rows.astype(jnp.float32)
    squares = lax.psum(jnp.sum(wide_ref * wide_ref, axis=1), "tp")
    own_inverse = jnp.sum(
        jnp.where(
            destination[:, None] == jnp.arange(replicas)[None, :], jnp.arange(replicas)[:, None], 0
        ),
        axis=0,
    )
    squares_sent = jnp.take(squares.reshape(replicas, block_rows), own_inverse, axis=0)
    square_in = lax.all_to_all(squares_sent, "rep", split_axis=0, concat_axis=0, tiled=True).reshape(-1)
    info, square_in, reference_rows, critic_rows = lax.optimization_barrier(
        (info, square_in, reference_rows, critic_rows)
    )

    split = lax.all_to_all(reference_rows, "tp", split_axis=0, concat_axis=1, tiled=True)
    slices = lax.all_to_all(split, "rep", split_axis=1, concat_axis=0, tiled=True)
    ref_slice = lax.all_gather(slices, "tp", axis=0, tiled=True)

    blocks = critic_rows.reshape(replicas, block_rows, -1)
    critic_sent = jnp.take(blocks, own_inverse, axis=0).reshape(critic_rows.shape)
    critic_in = lax.all_to_all(critic_sent, "rep", split_axis=0, concat_axis=0, tiled=True)

    ids_all, dest_all = info[:, :slot_count], info[:, slot_count:]
    inverse, received, valid, rank = tables(ids_all, dest_all)
    place = (rank[:, None, :] == jnp.arange(rows_per_pack)[None, :, None]) & valid[:, None, :]
    position = jnp.arange(slot_count)
    sender = position // block_rows
    in_sender = jnp.transpose(inverse)[:, :, None] * block_rows + jnp.arange(block_rows)[None, None, :]
    in_sender = in_sender.reshape(replicas, slot_count)
    row_of = (in_sender // quarter) * (replicas * quarter) + sender[None, :] * quarter + in_sender % quarter
    order = jnp.sum(jnp.where(place, row_of[:, None, :], 0), axis=2).reshape(-1)

    mine = lambda table: lax.dynamic_index_in_dim(table, me, 0, keepdims=False)
    place_mine = mine(place)
    chosen = jnp.sum(jnp.where(place_mine, position[None, :], 0), axis=1)
    pack_ids = jnp.sum(jnp.where(place_mine, mine(received)[None, :], 0), axis=1)

    compact = jnp.take(ref_slice, order, axis=0)
    weight = jnp.concatenate([ref_query, ref_key, ref_value], axis=1)
    partial = project(compact, weight).astype(jnp.bfloat16)
    parts = lax.all_to_all(partial, "rep", split_axis=0, concat_axis=0, tiled=True)

    critic_full = lax.all_gather(critic_in[chosen], "tp", axis=1, tiled=True)
    widened = critic_full.astype(jnp.float32)
    scale_row = lax.rsqrt(jnp.mean(widened * widened, axis=-1, keepdims=True) + 1e-05)
    critic_normed = (widened * scale_row).astype(jnp.bfloat16)
    critic_attn = attend(
        project(critic_normed, critic_query).astype(jnp.bfloat16),
        project(critic_normed, critic_key).astype(jnp.bfloat16),
        project(critic_normed, critic_value).astype(jnp.bfloat16),
        pack_ids,
    )

    square_rows = jnp.sum(jnp.where(place_mine, square_in[None, :], 0.0), axis=1) / (
        reference_rows.shape[1] * width
    )
    summed = jnp.sum(parts.reshape(replicas, rows_per_pack, -1).astype(jnp.float32), axis=0)
    ref_qkv = (summed * lax.rsqrt(square_rows + 1e-05)[:, None]).astype(jnp.bfloat16)
    nq, nk = ref_query.shape[1], ref_key.shape[1]
    ref_attn = attend(ref_qkv[:, :nq], ref_qkv[:, nq : nq + nk], ref_qkv[:, nq + nk :], pack_ids)

    terms = jnp.stack(
        [
            jnp.sum(ref_attn.astype(jnp.float32) * ref_readout.astype(jnp.float32), axis=1),
            jnp.sum(critic_attn.astype(jnp.float32) * critic_readout.astype(jnp.float32), axis=1),
        ]
    )
    spread = jnp.sum(jnp.where(place_mine[None, :, :], terms[:, :, None], 0.0), axis=1)
    spread = lax.psum(spread, "tp").reshape(2, replicas, block_rows)
    sent = jnp.transpose(spread, (1, 0, 2)).reshape(replicas, 2 * block_rows)
    back = lax.all_to_all(sent, "rep", split_axis=0, concat_axis=0, tiled=True)
    back = back.reshape(replicas, 2, block_rows)
    picked = destination[:, None] == jnp.arange(replicas)[None, :]
    home = jnp.sum(
        jnp.where(picked[:, :, None, None], back[None], 0.0), axis=1
    )
    home = jnp.transpose(home, (1, 0, 2)).reshape(2, slot_count)
    home = jnp.where(segment_ids[None, :] >= 0, home, 0.0)
    return (home[0], home[1])


def solution(mesh):
    return jax.shard_map(
        body,
        mesh=mesh,
        in_specs=(
            P("rep", "tp"),
            P("rep", "tp"),
            P("rep"),
            P("rep", None),
            P("rep", "tp"),
            P("rep", "tp"),
            P("rep", "tp"),
            P(None, "tp"),
            P(None, "tp"),
            P(None, "tp"),
            P("tp"),
            P("tp"),
        ),
        out_specs=(P("rep"), P("rep")),
        check_vma=False,
    )
```

```python
import jax
import jax.numpy as jnp
from jax import lax
from jax.sharding import PartitionSpec as P

HD = 128


def attend(queries, keys_in, values_in, segments):
    row_count = queries.shape[0]
    groups = keys_in.shape[1] // HD
    shared = queries.shape[1] // keys_in.shape[1]
    query_four = queries.reshape(row_count, groups, shared, HD)
    key_three = keys_in.reshape(row_count, groups, HD)
    value_three = values_in.reshape(row_count, groups, HD)
    scores = jnp.einsum(
        "pgjd,qgd->gjpq", query_four, key_three, preferred_element_type=jnp.float32
    ) * HD ** (-0.5)
    position = jnp.arange(row_count)
    allowed = (position[None, :] <= position[:, None]) & (segments[:, None] == segments[None, :])
    masked = jnp.where(allowed, scores, -1e30)
    row_max = jnp.max(masked, axis=-1, keepdims=True)
    powers = jnp.where(allowed, jnp.exp(masked - row_max), 0.0)
    weights = (powers / jnp.sum(powers, axis=-1, keepdims=True)).astype(jnp.bfloat16)
    mixture = jnp.einsum("gjpq,qgd->pgjd", weights, value_three, preferred_element_type=jnp.float32)
    return mixture.reshape(row_count, groups * shared * HD).astype(jnp.bfloat16)


def project(rows, weight):
    return jnp.dot(rows, weight, preferred_element_type=jnp.float32)


def tables(ids_all, dest_all):
    replicas = dest_all.shape[0]
    goes = dest_all[:, :, None] == jnp.arange(replicas)[None, None, :]
    inverse = jnp.sum(jnp.where(goes, jnp.arange(replicas)[None, :, None], 0), axis=1)
    ids_blocks = ids_all.reshape(replicas, replicas, -1)
    received = jnp.sum(
        jnp.where(goes[:, :, :, None], ids_blocks[:, :, None, :], 0), axis=1
    )
    received = jnp.transpose(received, (1, 0, 2)).reshape(replicas, -1)
    valid = received >= 0
    rank = jnp.cumsum(valid.astype(jnp.int32), axis=1) - 1
    return inverse, received, valid, rank


def body(
    reference_rows,
    critic_rows,
    segment_ids,
    pack_dest,
    ref_query,
    ref_key,
    ref_value,
    critic_query,
    critic_key,
    critic_value,
    ref_readout,
    critic_readout,
):
    replicas = lax.axis_size("rep")
    width = lax.axis_size("tp")
    me = lax.axis_index("rep")
    slot_count = segment_ids.shape[0]
    block_rows = slot_count // replicas
    rows_per_pack = slot_count // 2
    quarter = slot_count // width
    destination = pack_dest[0]

    own_info = jnp.concatenate([segment_ids, destination])
    copies = jnp.broadcast_to(own_info[None, :], (replicas, own_info.shape[0]))
    info = lax.all_to_all(copies, "rep", split_axis=0, concat_axis=0, tiled=True)
    wide_ref = reference_rows.astype(jnp.float32)
    squares = lax.psum(jnp.sum(wide_ref * wide_ref, axis=1), "tp")
    own_inverse = jnp.sum(
        jnp.where(
            destination[:, None] == jnp.arange(replicas)[None, :], jnp.arange(replicas)[:, None], 0
        ),
        axis=0,
    )
    squares_sent = jnp.take(squares.reshape(replicas, block_rows), own_inverse, axis=0)
    square_in = lax.all_to_all(squares_sent, "rep", split_axis=0, concat_axis=0, tiled=True).reshape(-1)

    split = lax.all_to_all(reference_rows, "tp", split_axis=0, concat_axis=1, tiled=True)
    slices = lax.all_to_all(split, "rep", split_axis=1, concat_axis=0, tiled=True)
    ref_slice = lax.all_gather(slices, "tp", axis=0, tiled=True)

    blocks = critic_rows.reshape(replicas, block_rows, -1)
    critic_sent = jnp.take(blocks, own_inverse, axis=0).reshape(critic_rows.shape)
    critic_in = lax.all_to_all(critic_sent, "rep", split_axis=0, concat_axis=0, tiled=True)

    ids_all, dest_all = info[:, :slot_count], info[:, slot_count:]
    inverse, received, valid, rank = tables(ids_all, dest_all)
    place = (rank[:, None, :] == jnp.arange(rows_per_pack)[None, :, None]) & valid[:, None, :]
    position = jnp.arange(slot_count)
    sender = position // block_rows
    in_sender = jnp.transpose(inverse)[:, :, None] * block_rows + jnp.arange(block_rows)[None, None, :]
    in_sender = in_sender.reshape(replicas, slot_count)
    row_of = (in_sender // quarter) * (replicas * quarter) + sender[None, :] * quarter + in_sender % quarter
    order = jnp.sum(jnp.where(place, row_of[:, None, :], 0), axis=2).reshape(-1)

    mine = lambda table: lax.dynamic_index_in_dim(table, me, 0, keepdims=False)
    place_mine = mine(place)
    chosen = jnp.sum(jnp.where(place_mine, position[None, :], 0), axis=1)
    pack_ids = jnp.sum(jnp.where(place_mine, mine(received)[None, :], 0), axis=1)

    compact = jnp.take(ref_slice, order, axis=0)
    weight = jnp.concatenate([ref_query, ref_key, ref_value], axis=1)
    partial = project(compact, weight).astype(jnp.bfloat16)
    parts = lax.all_to_all(partial, "rep", split_axis=0, concat_axis=0, tiled=True)

    critic_full = lax.all_gather(critic_in[chosen], "tp", axis=1, tiled=True)
    widened = critic_full.astype(jnp.float32)
    scale_row = lax.rsqrt(jnp.mean(widened * widened, axis=-1, keepdims=True) + 1e-05)
    critic_normed = (widened * scale_row).astype(jnp.bfloat16)
    critic_attn = attend(
        project(critic_normed, critic_query).astype(jnp.bfloat16),
        project(critic_normed, critic_key).astype(jnp.bfloat16),
        project(critic_normed, critic_value).astype(jnp.bfloat16),
        pack_ids,
    )

    square_rows = jnp.sum(jnp.where(place_mine, square_in[None, :], 0.0), axis=1) / (
        reference_rows.shape[1] * width
    )
    summed = jnp.sum(parts.reshape(replicas, rows_per_pack, -1).astype(jnp.float32), axis=0)
    ref_qkv = (summed * lax.rsqrt(square_rows + 1e-05)[:, None]).astype(jnp.bfloat16)
    nq, nk = ref_query.shape[1], ref_key.shape[1]
    ref_attn = attend(ref_qkv[:, :nq], ref_qkv[:, nq : nq + nk], ref_qkv[:, nq + nk :], pack_ids)

    terms = jnp.stack(
        [
            jnp.sum(ref_attn.astype(jnp.float32) * ref_readout.astype(jnp.float32), axis=1),
            jnp.sum(critic_attn.astype(jnp.float32) * critic_readout.astype(jnp.float32), axis=1),
        ]
    )
    spread = jnp.sum(jnp.where(place_mine[None, :, :], terms[:, :, None], 0.0), axis=1)
    spread = lax.psum(spread, "tp").reshape(2, replicas, block_rows)
    sent = jnp.transpose(spread, (1, 0, 2)).reshape(replicas, 2 * block_rows)
    back = lax.all_to_all(sent, "rep", split_axis=0, concat_axis=0, tiled=True)
    back = back.reshape(replicas, 2, block_rows)
    picked = destination[:, None] == jnp.arange(replicas)[None, :]
    home = jnp.sum(
        jnp.where(picked[:, :, None, None], back[None], 0.0), axis=1
    )
    home = jnp.transpose(home, (1, 0, 2)).reshape(2, slot_count)
    home = jnp.where(segment_ids[None, :] >= 0, home, 0.0)
    return (home[0], home[1])


def solution(mesh):
    return jax.shard_map(
        body,
        mesh=mesh,
        in_specs=(
            P("rep", "tp"),
            P("rep", "tp"),
            P("rep"),
            P("rep", None),
            P("rep", "tp"),
            P("rep", "tp"),
            P("rep", "tp"),
            P(None, "tp"),
            P(None, "tp"),
            P(None, "tp"),
            P("tp"),
            P("tp"),
        ),
        out_specs=(P("rep"), P("rep")),
        check_vma=False,
    )
```

```python
import jax
import jax.numpy as jnp
from jax import lax
from jax.sharding import PartitionSpec as P

HD = 128


def attend(queries, keys_in, values_in, segments):
    row_count = queries.shape[0]
    groups = keys_in.shape[1] // HD
    shared = queries.shape[1] // keys_in.shape[1]
    query_four = queries.reshape(row_count, groups, shared, HD)
    key_three = keys_in.reshape(row_count, groups, HD)
    value_three = values_in.reshape(row_count, groups, HD)
    scores = jnp.einsum(
        "pgjd,qgd->gjpq", query_four, key_three, preferred_element_type=jnp.float32
    ) * HD ** (-0.5)
    position = jnp.arange(row_count)
    allowed = (position[None, :] <= position[:, None]) & (segments[:, None] == segments[None, :])
    masked = jnp.where(allowed, scores, -1e30)
    row_max = jnp.max(masked, axis=-1, keepdims=True)
    powers = jnp.where(allowed, jnp.exp(masked - row_max), 0.0)
    weights = (powers / jnp.sum(powers, axis=-1, keepdims=True)).astype(jnp.bfloat16)
    mixture = jnp.einsum("gjpq,qgd->pgjd", weights, value_three, preferred_element_type=jnp.float32)
    return mixture.reshape(row_count, groups * shared * HD).astype(jnp.bfloat16)


def project(rows, weight):
    return jnp.dot(rows, weight, preferred_element_type=jnp.float32)


def tables(ids_all, dest_all):
    replicas = dest_all.shape[0]
    goes = dest_all[:, :, None] == jnp.arange(replicas)[None, None, :]
    inverse = jnp.sum(jnp.where(goes, jnp.arange(replicas)[None, :, None], 0), axis=1)
    ids_blocks = ids_all.reshape(replicas, replicas, -1)
    received = jnp.sum(
        jnp.where(goes[:, :, :, None], ids_blocks[:, :, None, :], 0), axis=1
    )
    received = jnp.transpose(received, (1, 0, 2)).reshape(replicas, -1)
    valid = received >= 0
    rank = jnp.cumsum(valid.astype(jnp.int32), axis=1) - 1
    return inverse, received, valid, rank


def body(
    reference_rows,
    critic_rows,
    segment_ids,
    pack_dest,
    ref_query,
    ref_key,
    ref_value,
    critic_query,
    critic_key,
    critic_value,
    ref_readout,
    critic_readout,
):
    replicas = lax.axis_size("rep")
    width = lax.axis_size("tp")
    me = lax.axis_index("rep")
    slot_count = segment_ids.shape[0]
    block_rows = slot_count // replicas
    rows_per_pack = slot_count // 2
    quarter = slot_count // width
    destination = pack_dest[0]

    own_info = jnp.concatenate([segment_ids, destination])
    copies = jnp.broadcast_to(own_info[None, :], (replicas, own_info.shape[0]))
    info = lax.all_to_all(copies, "rep", split_axis=0, concat_axis=0, tiled=True)
    wide_ref = reference_rows.astype(jnp.float32)
    squares = lax.psum(jnp.sum(wide_ref * wide_ref, axis=1), "tp")
    own_inverse = jnp.sum(
        jnp.where(
            destination[:, None] == jnp.arange(replicas)[None, :], jnp.arange(replicas)[:, None], 0
        ),
        axis=0,
    )
    squares_sent = jnp.take(squares.reshape(replicas, block_rows), own_inverse, axis=0)
    square_in = lax.all_to_all(squares_sent, "rep", split_axis=0, concat_axis=0, tiled=True).reshape(-1)

    split = lax.all_to_all(reference_rows, "tp", split_axis=0, concat_axis=1, tiled=True)
    slices = lax.all_to_all(split, "rep", split_axis=1, concat_axis=0, tiled=True)
    ref_slice = lax.all_gather(slices, "tp", axis=0, tiled=True)

    blocks = critic_rows.reshape(replicas, block_rows, -1)
    critic_sent = jnp.take(blocks, own_inverse, axis=0).reshape(critic_rows.shape)
    critic_in = lax.all_to_all(critic_sent, "rep", split_axis=0, concat_axis=0, tiled=True)

    ids_all, dest_all = info[:, :slot_count], info[:, slot_count:]
    inverse, received, valid, rank = tables(ids_all, dest_all)
    place = (rank[:, None, :] == jnp.arange(rows_per_pack)[None, :, None]) & valid[:, None, :]
    position = jnp.arange(slot_count)
    sender = position // block_rows
    in_sender = jnp.transpose(inverse)[:, :, None] * block_rows + jnp.arange(block_rows)[None, None, :]
    in_sender = in_sender.reshape(replicas, slot_count)
    row_of = (in_sender // quarter) * (replicas * quarter) + sender[None, :] * quarter + in_sender % quarter
    order = jnp.sum(jnp.where(place, row_of[:, None, :], 0), axis=2).reshape(-1)

    mine = lambda table: lax.dynamic_index_in_dim(table, me, 0, keepdims=False)
    place_mine = mine(place)
    chosen = jnp.sum(jnp.where(place_mine, position[None, :], 0), axis=1)
    pack_ids = jnp.sum(jnp.where(place_mine, mine(received)[None, :], 0), axis=1)

    pick = (order[:, None] == jnp.arange(ref_slice.shape[0])[None, :]).astype(jnp.bfloat16)
    compact = project(pick, ref_slice).astype(jnp.bfloat16)
    weight = jnp.concatenate([ref_query, ref_key, ref_value], axis=1)
    partial = project(compact, weight).astype(jnp.bfloat16)
    parts = lax.all_to_all(partial, "rep", split_axis=0, concat_axis=0, tiled=True)

    critic_full = lax.all_gather(critic_in[chosen], "tp", axis=1, tiled=True)
    widened = critic_full.astype(jnp.float32)
    scale_row = lax.rsqrt(jnp.mean(widened * widened, axis=-1, keepdims=True) + 1e-05)
    critic_normed = (widened * scale_row).astype(jnp.bfloat16)
    critic_attn = attend(
        project(critic_normed, critic_query).astype(jnp.bfloat16),
        project(critic_normed, critic_key).astype(jnp.bfloat16),
        project(critic_normed, critic_value).astype(jnp.bfloat16),
        pack_ids,
    )

    square_rows = jnp.sum(jnp.where(place_mine, square_in[None, :], 0.0), axis=1) / (
        reference_rows.shape[1] * width
    )
    summed = jnp.sum(parts.reshape(replicas, rows_per_pack, -1).astype(jnp.float32), axis=0)
    ref_qkv = (summed * lax.rsqrt(square_rows + 1e-05)[:, None]).astype(jnp.bfloat16)
    nq, nk = ref_query.shape[1], ref_key.shape[1]
    ref_attn = attend(ref_qkv[:, :nq], ref_qkv[:, nq : nq + nk], ref_qkv[:, nq + nk :], pack_ids)

    terms = jnp.stack(
        [
            jnp.sum(ref_attn.astype(jnp.float32) * ref_readout.astype(jnp.float32), axis=1),
            jnp.sum(critic_attn.astype(jnp.float32) * critic_readout.astype(jnp.float32), axis=1),
        ]
    )
    spread = jnp.sum(jnp.where(place_mine[None, :, :], terms[:, :, None], 0.0), axis=1)
    spread = lax.psum(spread, "tp").reshape(2, replicas, block_rows)
    sent = jnp.transpose(spread, (1, 0, 2)).reshape(replicas, 2 * block_rows)
    back = lax.all_to_all(sent, "rep", split_axis=0, concat_axis=0, tiled=True)
    back = back.reshape(replicas, 2, block_rows)
    picked = destination[:, None] == jnp.arange(replicas)[None, :]
    home = jnp.sum(
        jnp.where(picked[:, :, None, None], back[None], 0.0), axis=1
    )
    home = jnp.transpose(home, (1, 0, 2)).reshape(2, slot_count)
    home = jnp.where(segment_ids[None, :] >= 0, home, 0.0)
    return (home[0], home[1])


def solution(mesh):
    return jax.shard_map(
        body,
        mesh=mesh,
        in_specs=(
            P("rep", "tp"),
            P("rep", "tp"),
            P("rep"),
            P("rep", None),
            P("rep", "tp"),
            P("rep", "tp"),
            P("rep", "tp"),
            P(None, "tp"),
            P(None, "tp"),
            P(None, "tp"),
            P("tp"),
            P("tp"),
        ),
        out_specs=(P("rep"), P("rep")),
        check_vma=False,
    )
```
